128 devices in a mesh: blk: 16 (over y, x_hi, core), head: 8 (over x_lo, z).
Axes of the slice: x: 4 (x_hi: 2, x_lo: 2; x = x_hi * 2 + x_lo), y: 4, z: 4, core: 2. Of those that a mesh axis runs over, the one named last changes fastest.
Arguments:
- query: bfloat16 [16384, 4096], P(('blk', 'head')), may hold values from -10 to 10
- keys: bfloat16 [16384, 1024], P(('blk', 'head')), may hold values from -10 to 10
- values: bfloat16 [16384, 1024], P(('blk', 'head')), may hold values from -6 to 6
- positions: int32 [16384], P('blk'), may hold values from 0 to 16383, as said below
Outputs:
- attended: bfloat16 [16384, 4096], P(('blk', 'head'))
The draws below stay inside these ranges and needn't reach their ends.
Inputs may be any that keep to these rules, and one draw needn't show every extreme that they name: positions is a permutation of 0 .. 16383 made of aligned segments of 512 stored rows, each holding 512 consecutive positions in increasing order.
All inputs are finite; a program needn't handle non-finite values.
Results may differ from the reference program's by a relative error of at most 0.0065.
Values may be sent and summed in bfloat16 or wider, within the bound.
No kernel may reach another device: no remote copies, remote signals or barrier semaphores. Data moves between devices by JAX's collectives and lax.ppermute only.
A program may use at most 128 MiB of HBM per device.

```python
import jax
import jax.numpy as jnp
from jax import lax

HEADS = 32
KV_HEADS = 8
HEAD_DIM = 128
SEQ = 16384
SEGLEN = 512
KVWIDTH = 1024


def draw_query(key, part):
    key = jax.random.fold_in(key, 1)
    return jnp.clip(jax.random.normal(key, (SEQ, HEADS * HEAD_DIM), jnp.float32), -6.0, 6.0).astype(jnp.bfloat16)


def draw_keys(key, part):
    key = jax.random.fold_in(key, 2)
    return jnp.clip(jax.random.normal(key, (SEQ, KV_HEADS * HEAD_DIM), jnp.float32), -6.0, 6.0).astype(jnp.bfloat16)


def draw_positions(key, part):
    key = jax.random.fold_in(key, 3)
    order = jax.random.permutation(key, SEQ // SEGLEN).astype(jnp.int32)
    rows = jnp.arange(SEQ, dtype=jnp.int32)
    return order[rows // SEGLEN] * SEGLEN + rows % SEGLEN


def block_levels(key, dims, cuts, low, top_value):
    gain, own = 1.0, jax.random.fold_in(key, 6)
    for position, parts in cuts:
        heights = jnp.exp(jax.random.uniform(jax.random.fold_in(own, position), (parts,), jnp.float32, low / len(cuts), top_value / len(cuts)))
        gain = gain * jnp.repeat(heights, dims[position] // parts).reshape([-1 if axis == position else 1 for axis in range(len(dims))])
    return gain


def normal_values(own_key, dims, scale, reach, cuts=(), kind=jnp.bfloat16):
    gain = block_levels(own_key, dims, cuts, -0.22, 0.18) if cuts else 1.0
    drawn = jax.random.normal(own_key, dims, jnp.float32) * scale * gain
    return jnp.minimum(jnp.maximum(drawn, -reach), reach).astype(kind)


def setup_inputs(seed: int = 0) -> dict:
    splits = jax.random.split(jax.random.key(seed), 5)
    query = draw_query(jax.random.fold_in(splits[4], 71), 0)
    keys = draw_keys(jax.random.fold_in(splits[4], 71), 0)
    values = normal_values(splits[2], (SEQ, KVWIDTH), 1.0, 6.0, ((0, 128),))
    positions = draw_positions(jax.random.fold_in(splits[4], 71), 0)
    return {"query": query, "keys": keys, "values": values, "positions": positions}


def reference(query, keys, values, positions):
    group = HEADS // KV_HEADS
    scale = HEAD_DIM ** -0.5
    key_all = keys.astype(jnp.float32).reshape(SEQ, KV_HEADS, HEAD_DIM)
    val_all = values.astype(jnp.float32).reshape(SEQ, KV_HEADS, HEAD_DIM)
    block = 256 if SEQ % 256 == 0 else SEQ

    def one_block(index):
        start = (index * block).astype(jnp.int32)
        q_block = lax.dynamic_slice_in_dim(query, start, block, 0).astype(jnp.float32)
        q_block = q_block.reshape(block, KV_HEADS, group, HEAD_DIM)
        q_pos = lax.dynamic_slice_in_dim(positions, start, block, 0)
        visible = positions[None, :] <= q_pos[:, None]

        def one_head(hindex):
            q_head = lax.dynamic_index_in_dim(q_block, hindex, 1, keepdims=False)
            k_head = lax.dynamic_index_in_dim(key_all, hindex, 1, keepdims=False)
            v_head = lax.dynamic_index_in_dim(val_all, hindex, 1, keepdims=False)
            scores = jnp.einsum("rgd,sd->grs", q_head, k_head) * scale
            scores = jnp.where(visible[None], scores, -jnp.inf)
            top = jnp.max(scores, axis=-1, keepdims=True)
            weights = jnp.exp(scores - top)
            total = jnp.sum(weights, axis=-1)
            probs = lax.optimization_barrier(weights.astype(jnp.bfloat16)).astype(jnp.float32)
            summed = jnp.einsum("grs,sd->rgd", probs, v_head)
            return summed / jnp.transpose(total)[:, :, None]

        outs = lax.map(one_head, jnp.arange(KV_HEADS, dtype=jnp.int32))
        return jnp.transpose(outs, (1, 0, 2, 3)).reshape(block, HEADS * HEAD_DIM)

    result = lax.map(one_block, jnp.arange(SEQ // block, dtype=jnp.int32))
    return result.reshape(SEQ, HEADS * HEAD_DIM).astype(jnp.bfloat16)
```

```python
import functools

import jax
import jax.numpy as jnp
from jax import lax
from jax.experimental import pallas as pl
from jax.experimental.pallas import tpu as pltpu
from jax.sharding import PartitionSpec as P

HEADS = 32
KV_HEADS = 8
HEAD_DIM = 128
GROUP = HEADS // KV_HEADS
SEGLEN = 512
SEGS = 32
PART = SEGLEN // 16
TILE = GROUP * PART
ROWS = SEGS * TILE
QB = 512
QSEGS = QB // TILE
QBLOCKS = ROWS // QB
LOG2E = 1.4426950408889634
SCALE = HEAD_DIM**-0.5 * LOG2E
LOW = -1e30
UNROLL = 4
NT = (((1,), (1,)), ((), ()))
bf16, f32, i32 = jnp.bfloat16, jnp.float32, jnp.int32


def attend(sizes, first, last, *refs):
    n_seg = sum(sizes)
    refs = list(refs)
    meta, q_ref = refs[:2]
    refs = refs[2:]
    state_in = None if first else refs.pop(0)
    chunks, refs = refs[: len(sizes)], refs[len(sizes) :]
    if first:
        qs, state_out = refs[:2]
        refs = refs[2:]
    elif last:
        qs, out = q_ref, refs.pop(0)
    else:
        qs, state_out = q_ref, refs.pop(0)
    kv, m_ref, l_ref, acc, s_scr, p_scr, a_scr, base, st_e, st_r, st_p, sems = refs
    state = (m_ref, l_ref, acc)

    copies, start = [], 0
    for index, size in enumerate(sizes):
        copies.append(pltpu.make_async_copy(chunks[index], kv.at[pl.ds(start, size)], sems.at[index]))
        start += size
    if not first:
        for index, ref in enumerate(state):
            copies.append(
                pltpu.make_async_copy(state_in.at[index], ref.at[pl.ds(0, ROWS)], sems.at[len(sizes) + index])
            )
    for copy in copies:
        copy.start()

    def masked_step(e, _):
        p = meta[meta[SEGS + e]]
        st_e[1 + e] = e
        st_r[1 + e] = lax.div(p, QSEGS)
        st_p[1 + e] = p
        return 0

    lax.fori_loop(0, n_seg, masked_step, 0)

    def full_steps(e, count):
        def one(r, count):
            st_e[count] = e
            st_r[count] = r
            return count + 1

        return lax.fori_loop(st_r[1 + e] + 1, QBLOCKS, one, count)

    count = lax.fori_loop(0, n_seg, full_steps, 1 + n_seg)
    for index in [0] + [count + i for i in range(UNROLL + 2)]:
        st_e[index] = 0
        st_r[index] = QBLOCKS

    row = lax.broadcasted_iota(i32, (QB, 128), 0)
    lane = lax.broadcasted_iota(i32, (QB, 128), 1)
    within = lax.rem(row, TILE)
    place = lax.rem(within, PART)
    base[...] = (
        lax.div(row, TILE) * SEGLEN + lax.div(place, 8) * 128 + lax.rem(place, 8) + meta[2 * SEGS] - lane
    )

    if first:
        def stack(s, _):
            p = meta[s]
            for g in range(GROUP):
                to = pl.multiple_of(p * TILE + g * PART, PART)
                qs[pl.ds(to, PART), :] = q_ref[
                    pl.ds(pl.multiple_of(s * PART, PART), PART), g * HEAD_DIM : (g + 1) * HEAD_DIM
                ]
            return 0

        lax.fori_loop(0, SEGS, stack, 0)
        qs[pl.ds(ROWS, QB), :] = jnp.zeros((QB, HEAD_DIM), bf16)
        m_ref[...] = jnp.full_like(m_ref, LOW)
        l_ref[...] = jnp.zeros_like(l_ref)
        acc[...] = jnp.zeros_like(acc)
    p_scr[0] = jnp.zeros((QB, SEGLEN), bf16)
    a_scr[0] = jnp.zeros((QB, 128), f32)

    for copy in copies:
        copy.wait()

    def rows_of(t):
        return pl.ds(pl.multiple_of(st_r[t] * QB, QB), QB)

    def scores(t, slot):
        s_scr[slot] = lax.dot_general(
            qs[rows_of(t), :], kv[st_e[t], :, :HEAD_DIM], NT, preferred_element_type=f32
        )

    def soften(t, slot, masked):
        rows = rows_of(t)
        pieces = range(0, SEGLEN, 128)
        if masked:
            shift = (st_p[t] - st_r[t] * QSEGS) * SEGLEN
            for c in pieces:
                s_scr[slot, :, c : c + 128] = jnp.where(
                    base[...] >= shift + c, s_scr[slot, :, c : c + 128], LOW
                )
        top = s_scr[slot, :, 0:128]
        for c in pieces[1:]:
            top = jnp.maximum(top, s_scr[slot, :, c : c + 128])
        before = m_ref[rows, :]
        now = jnp.maximum(before, jnp.max(top, axis=1, keepdims=True) * SCALE)
        factor = jnp.exp2(before - now)
        m_ref[rows, :] = now
        a_scr[slot] = factor
        total = l_ref[rows, :] * factor
        for c in pieces:
            weight = jnp.exp2(s_scr[slot, :, c : c + 128] * SCALE - now)
            total = total + weight
            p_scr[slot, :, c : c + 128] = weight.astype(bf16)
        l_ref[rows, :] = total

    def gather(t, slot):
        rows = rows_of(t)
        added = jnp.dot(p_scr[slot], kv[st_e[t], :, HEAD_DIM:], preferred_element_type=f32)
        acc[rows, :] = acc[rows, :] * a_scr[slot] + added

    def steps(masked, offset):
        def body(u, _):
            for r in range(UNROLL):
                t = offset + u * UNROLL + r
                slot = (offset + r) % 2
                gather(t - 1, 1 - slot)
                soften(t, slot, masked)
                scores(t + 1, 1 - slot)
            return 0

        return body

    assert n_seg % UNROLL == 0
    scores(1, 1)
    lax.fori_loop(0, n_seg // UNROLL, steps(True, 1), 0)
    left = count - n_seg
    lax.fori_loop(0, lax.div(left + UNROLL - 1, UNROLL), steps(False, 1 + n_seg), 0)

    if last:
        def finish(s, _):
            p = meta[s]
            for g in range(GROUP):
                rows = pl.ds(pl.multiple_of(p * TILE + g * PART, PART), PART)
                total = jnp.sum(l_ref[rows, :], axis=1, keepdims=True)
                out[pl.ds(pl.multiple_of(s * PART, PART), PART), g * HEAD_DIM : (g + 1) * HEAD_DIM] = (
                    acc[rows, :] / total
                ).astype(bf16)
            return 0

        lax.fori_loop(0, SEGS, finish, 0)
    else:
        copies = [
            pltpu.make_async_copy(ref.at[pl.ds(0, ROWS)], state_out.at[index], sems.at[index])
            for index, ref in enumerate(state)
        ]
        for copy in copies:
            copy.start()
        for copy in copies:
            copy.wait()


def attention_call(order, mine, blocks, q, state, chunks, last):
    first = state is None
    chunks = [c.reshape(-1, SEGLEN, 2 * HEAD_DIM) for c in chunks]
    sizes = [c.shape[0] for c in chunks]
    n_seg = sum(sizes)
    segments = jnp.stack([jnp.stack([2 * b, 2 * b + 1]) for b in blocks]).reshape(-1)
    segments = jnp.pad(segments, (0, SEGS - n_seg))
    meta = jnp.concatenate([order, segments, jnp.full((8,), mine * 8, i32)])
    vmem, hbm = pl.BlockSpec(memory_space=pltpu.VMEM), pl.BlockSpec(memory_space=pl.ANY)
    operands = [meta, q] + ([] if first else [state]) + chunks
    in_specs = [pl.BlockSpec(memory_space=pltpu.SMEM), vmem] + [hbm] * (len(operands) - 2)
    stacked = jax.ShapeDtypeStruct((ROWS + QB, HEAD_DIM), bf16)
    saved = jax.ShapeDtypeStruct((3, ROWS, 128), f32)
    if first:
        out_shape, out_specs = (stacked, saved), (vmem, hbm)
    elif last:
        out_shape, out_specs = jax.ShapeDtypeStruct((SEGS * PART, GROUP * HEAD_DIM), bf16), vmem
    else:
        out_shape, out_specs = saved, hbm
    steps = n_seg * 9 // 2 + n_seg // 2
    return pl.pallas_call(
        functools.partial(attend, sizes, first, last),
        out_shape=out_shape,
        in_specs=in_specs,
        out_specs=out_specs,
        scratch_shapes=[
            pltpu.VMEM((n_seg, SEGLEN, 2 * HEAD_DIM), bf16),
            pltpu.VMEM((ROWS + QB, 128), f32),
            pltpu.VMEM((ROWS + QB, 128), f32),
            pltpu.VMEM((ROWS + QB, 128), f32),
            pltpu.VMEM((2, QB, SEGLEN), f32),
            pltpu.VMEM((2, QB, SEGLEN), bf16),
            pltpu.VMEM((2, QB, 128), f32),
            pltpu.VMEM((QB, 128), i32),
            pltpu.SMEM((n_seg * (QBLOCKS + 1) + 16,), i32),
            pltpu.SMEM((n_seg * (QBLOCKS + 1) + 16,), i32),
            pltpu.SMEM((n_seg * (QBLOCKS + 1) + 16,), i32),
            pltpu.SemaphoreType.DMA((len(sizes) + 3,)),
        ],
        compiler_params=pltpu.CompilerParams(vmem_limit_bytes=40 * 2**20),
        cost_estimate=pl.CostEstimate(
            flops=steps * QB * SEGLEN * 4 * HEAD_DIM,
            bytes_accessed=n_seg * SEGLEN * 512 + ROWS * 128 * 24,
            transcendentals=steps * QB * SEGLEN,
        ),
    )(*operands)


def moved(x, dy, dx, dcore):
    pairs = []
    for y in range(4):
        for x_hi in range(2):
            for core in range(2):
                to = ((y + dy) % 4) * 4 + (x_hi ^ dx) * 2 + (core ^ dcore)
                pairs.append((y * 4 + x_hi * 2 + core, to))
    return lax.ppermute(x, "blk", pairs)


def per_device(query, keys, values, positions):
    n_blk, n_head = lax.axis_size("blk"), lax.axis_size("head")
    blk, head = lax.axis_index("blk"), lax.axis_index("head")
    rows = query.shape[0]
    quarters = SEGLEN // rows

    both = jnp.concatenate(
        [keys.reshape(rows, n_head, HEAD_DIM), values.reshape(rows, n_head, HEAD_DIM)], axis=2
    )
    own = lax.all_to_all(jnp.transpose(both, (1, 0, 2)), "head", split_axis=0, concat_axis=0, tiled=True)
    own = own.reshape(n_head * rows, 2 * HEAD_DIM)

    per = rows // n_blk
    q_out = jnp.transpose(query.reshape(n_blk, per, n_head, GROUP * HEAD_DIM), (0, 2, 1, 3))
    place = lax.dynamic_index_in_dim(positions, lax.div(head, quarters) * SEGLEN, 0, keepdims=False)
    place = lax.div(place, SEGLEN).astype(bf16)
    tag = jnp.full((n_blk, n_head, per, 128), place, bf16)
    q_out = jnp.concatenate([q_out, tag], axis=3).reshape(n_blk * n_head, per, GROUP * HEAD_DIM + 128)
    q_in = lax.all_to_all(q_out, ("blk", "head"), split_axis=0, concat_axis=0, tiled=True)
    order = q_in[::quarters, 0, GROUP * HEAD_DIM].astype(i32)
    q_in = q_in.reshape(n_blk * n_head * per, GROUP * HEAD_DIM + 128)

    half = n_head * rows
    near = jnp.concatenate([own, moved(own, 0, 1, 0)], axis=0)
    near_core = moved(near, 0, 0, 1)
    up, down = moved(near, 1, 0, 0), moved(near, -1, 0, 0)
    up_core, down_core = moved(up, 0, 0, 1), moved(down, 0, 0, 1)
    far_up, far_down = moved(up[:half], 1, 0, 0), moved(down[half:], -1, 0, 0)
    far_up_core, far_down_core = moved(far_up, 0, 0, 1), moved(far_down, 0, 0, 1)

    def of(dy, dx, dcore):
        return lax.rem(blk + 4 * dy + n_blk, n_blk) ^ (2 * dx + dcore)

    stacked, state = attention_call(
        order, blk, [of(0, 0, 0), of(0, 1, 0), of(0, 0, 1), of(0, 1, 1)], q_in, None, [near, near_core], False
    )
    state = attention_call(
        order,
        blk,
        [of(-1, 0, 0), of(-1, 1, 0), of(1, 0, 0), of(1, 1, 0), of(-1, 0, 1), of(-1, 1, 1), of(1, 0, 1), of(1, 1, 1)],
        stacked,
        state,
        [up, down, up_core, down_core],
        False,
    )
    out = attention_call(
        order,
        blk,
        [of(2, 0, 0), of(2, 1, 0), of(2, 0, 1), of(2, 1, 1)],
        stacked,
        state,
        [far_up, far_down, far_up_core, far_down_core],
        True,
    )
    out = out.reshape(n_blk * n_head, per, GROUP * HEAD_DIM)
    back = lax.all_to_all(out, ("blk", "head"), split_axis=0, concat_axis=0, tiled=True)
    back = back.reshape(n_blk, n_head, per, GROUP * HEAD_DIM)
    return jnp.transpose(back, (0, 2, 1, 3)).reshape(rows, HEADS * HEAD_DIM)


def solution(mesh):
    placed = (
        P(("blk", "head"), None),
        P(("blk", "head"), None),
        P(("blk", "head"), None),
        P("blk"),
    )
    return jax.shard_map(
        per_device, mesh=mesh, in_specs=placed, out_specs=P(("blk", "head"), None), check_vma=False
    )
```

```python
import functools

import jax
import jax.numpy as jnp
import numpy as np
from jax import lax
from jax.experimental import pallas as pl
from jax.experimental.pallas import tpu as pltpu
from jax.sharding import PartitionSpec as P

HEADS = 32
KV_HEADS = 8
HEAD_DIM = 128
GROUP = HEADS // KV_HEADS
SEGLEN = 512
SEGS = 32
PART = SEGLEN // 16
TILE = GROUP * PART
ROWS = SEGS * TILE
QSEGS = 4
QB = QSEGS * TILE
BLOCKS = SEGS // QSEGS
UNROLL = 4
WIDE = 2 * HEAD_DIM
LOG2E = 1.4426950408889634
SCALE = HEAD_DIM**-0.5 * LOG2E
SAFE = 48.0
LOW = -1e30
NT = (((1,), (1,)), ((), ()))
bf16, f32, i32 = jnp.bfloat16, jnp.float32, jnp.int32

STEPS = [(b, b) for b in range(BLOCKS)] + [(q, k) for k in range(BLOCKS) for q in range(k + 1, BLOCKS)]


def attend(n, done, first, last, *refs):
    refs = list(refs)
    meta, q_ref = refs[:2]
    refs = refs[2:]
    if not first:
        acc_in, m_in = refs[:2]
        refs = refs[2:]
    chunks, refs = refs[:n], refs[n:]
    qs = refs.pop(0) if first else q_ref
    acc, m_out = refs[:2]
    refs = refs[2:]
    if last:
        out = refs.pop(0)
    kv, m_ref, s_scr, p_scr, q_pos, k_pos, m_sem = refs
    shifted = meta[SEGS]
    part = n * PART
    keys = QSEGS * part

    row = lax.broadcasted_iota(i32, (QB, 128), 0)
    place = lax.rem(row, PART)
    q_pos[...] = lax.div(row, TILE) * SEGLEN + lax.div(place, 8) * 128 + lax.rem(place, 8) + meta[SEGS + 1]
    column = lax.broadcasted_iota(i32, (8, keys), 1)
    within = sum(jnp.where(column >= i * part, 1, 0) for i in range(1, QSEGS))
    chunk = column - within * part
    offset = sum(jnp.where(lax.div(chunk, PART) == c, meta[SEGS + 8 + 2 * len(STEPS) + done + c], 0) for c in range(n))
    place = lax.rem(chunk, PART)
    k_pos[...] = within * SEGLEN + lax.div(place, 8) * 128 + lax.rem(place, 8) + offset
    kv[:, :, WIDE:] = jnp.ones((BLOCKS, keys, HEAD_DIM), bf16)

    def lay(s, _):
        p = meta[s]
        block, within = lax.div(p, QSEGS), lax.rem(p, QSEGS)
        rows = pl.ds(pl.multiple_of(s * PART, PART), PART)
        for c in range(n):
            to = pl.ds(pl.multiple_of(within * part + c * PART, PART), PART)
            kv[block, to, :WIDE] = chunks[c][rows, :]
        if first:
            for g in range(GROUP):
                to = pl.ds(pl.multiple_of(p * TILE + g * PART, PART), PART)
                qs[to, :] = q_ref[rows, g * HEAD_DIM : (g + 1) * HEAD_DIM]
        return 0

    lax.fori_loop(0, SEGS, lay, 0)

    def step_of(t):
        if isinstance(t, int):
            return STEPS[t]
        return meta[SEGS + 8 + t], meta[SEGS + 8 + len(STEPS) + t]

    def rows_of(block):
        return pl.ds(pl.multiple_of(block * QB, QB), QB)

    def scores(t):
        q_block, k_block = step_of(t)
        return lax.dot_general(
            qs[rows_of(q_block), :], kv[k_block, :, :HEAD_DIM], NT, preferred_element_type=f32
        )

    def seen(c):
        return k_pos[0:1, c : c + 128] <= q_pos[...]

    def weigh(t, slot, masked):
        weights = jnp.exp2(scores(t) * SCALE)
        if masked:
            for c in range(0, keys, 128):
                kept = jnp.where(seen(c), weights[:, c : c + 128], 0.0)
                p_scr[slot, :, c : c + 128] = kept.astype(bf16)
        else:
            p_scr[slot] = weights.astype(bf16)

    def collect(t, slot):
        return jnp.dot(p_scr[slot], kv[step_of(t)[1], :, HEAD_DIM:], preferred_element_type=f32)

    @pl.when(shifted == 0)
    def _():
        for t in range(BLOCKS):
            weigh(t, t % 2, True)
            if t:
                rows = rows_of(t - 1)
                added = collect(t - 1, (t - 1) % 2)
                acc[rows, :] = added if first else acc_in[rows, :] + added

        rows, added = rows_of(BLOCKS - 1), collect(BLOCKS - 1, (BLOCKS - 1) % 2)
        acc[rows, :] = added if first else acc_in[rows, :] + added
        weigh(BLOCKS, 0, False)

        def body(u, _):
            for r in range(UNROLL):
                t = BLOCKS + u * UNROLL + r
                weigh(jnp.minimum(t + 1, len(STEPS) - 1), (r + 1) % 2, False)
                acc[rows_of(step_of(t)[0]), :] += collect(t, r % 2)
            return 0

        assert (len(STEPS) - BLOCKS) % UNROLL == 0
        lax.fori_loop(0, (len(STEPS) - BLOCKS) // UNROLL, body, 0)

    @pl.when(shifted != 0)
    def _():
        if first:
            m_ref[...] = jnp.full_like(m_ref, LOW)
            acc[...] = jnp.zeros_like(acc)
        else:
            copy = pltpu.make_async_copy(m_in, m_ref, m_sem)
            copy.start()
            copy.wait()
            acc[...] = acc_in[...]

        def step(masked):
            def body(t, _):
                rows = rows_of(step_of(t)[0])
                s_scr[...] = scores(t) * SCALE
                if masked:
                    for c in range(0, keys, 128):
                        s_scr[:, c : c + 128] = jnp.where(seen(c), s_scr[:, c : c + 128], LOW)
                before = m_ref[rows, :]
                now = jnp.maximum(before, jnp.max(s_scr[...], axis=1, keepdims=True))
                factor = jnp.exp2(before - now)
                m_ref[rows, :] = now
                for c in range(0, keys, 128):
                    p_scr[0, :, c : c + 128] = jnp.exp2(s_scr[:, c : c + 128] - now).astype(bf16)
                added = collect(t, 0)
                for c in (0, HEAD_DIM):
                    to = slice(c, c + HEAD_DIM)
                    acc[rows, to] = acc[rows, to] * factor + added[:, to]
                return 0

            return body

        lax.fori_loop(0, BLOCKS, step(True), 0)
        lax.fori_loop(BLOCKS, len(STEPS), step(False), 0)
        copy = pltpu.make_async_copy(m_ref, m_out, m_sem)
        copy.start()
        copy.wait()

    if last:
        def finish(s, _):
            p = meta[s]
            for g in range(GROUP):
                rows = pl.ds(pl.multiple_of(p * TILE + g * PART, PART), PART)
                out[pl.ds(pl.multiple_of(s * PART, PART), PART), g * HEAD_DIM : (g + 1) * HEAD_DIM] = (
                    acc[rows, :HEAD_DIM] / acc[rows, HEAD_DIM:]
                ).astype(bf16)
            return 0

        lax.fori_loop(0, SEGS, finish, 0)


def attention_call(meta, done, q, state, chunks, last):
    first, n = state is None, len(chunks)
    keys = QSEGS * n * PART
    vmem, hbm = pl.BlockSpec(memory_space=pltpu.VMEM), pl.BlockSpec(memory_space=pl.ANY)
    smem = pl.BlockSpec(memory_space=pltpu.SMEM)
    operands = [meta, q] + ([] if first else list(state)) + chunks
    in_specs = [smem, vmem] + ([] if first else [vmem, hbm]) + [vmem] * n
    out_shape = [jax.ShapeDtypeStruct((ROWS, WIDE), f32), jax.ShapeDtypeStruct((ROWS, 128), f32)]
    out_specs = [vmem, hbm]
    if first:
        out_shape = [jax.ShapeDtypeStruct((ROWS, HEAD_DIM), bf16)] + out_shape
        out_specs = [vmem] + out_specs
    if last:
        out_shape = out_shape + [jax.ShapeDtypeStruct((SEGS * PART, GROUP * HEAD_DIM), bf16)]
        out_specs = out_specs + [vmem]
    return pl.pallas_call(
        functools.partial(attend, n, done, first, last),
        out_shape=tuple(out_shape),
        in_specs=in_specs,
        out_specs=tuple(out_specs),
        input_output_aliases={} if first else {2: 0},
        scratch_shapes=[
            pltpu.VMEM((BLOCKS, keys, WIDE + HEAD_DIM), bf16),
            pltpu.VMEM((ROWS, 128), f32),
            pltpu.VMEM((QB, keys), f32),
            pltpu.VMEM((2, QB, keys), bf16),
            pltpu.VMEM((QB, 128), i32),
            pltpu.VMEM((8, keys), i32),
            pltpu.SemaphoreType.DMA,
        ],
        compiler_params=pltpu.CompilerParams(vmem_limit_bytes=36 * 2**20),
        cost_estimate=pl.CostEstimate(
            flops=len(STEPS) * QB * keys * 4 * WIDE,
            bytes_accessed=n * SEGS * PART * 512 + ROWS * WIDE * 4,
            transcendentals=len(STEPS) * QB * keys,
        ),
    )(*operands)


def held(step, *arrays):
    hbm = pl.BlockSpec(memory_space=pl.ANY)

    def nothing(*refs):
        del refs

    return pl.pallas_call(
        nothing,
        out_shape=tuple(jax.ShapeDtypeStruct(a.shape, a.dtype) for a in arrays),
        in_specs=[hbm] * (1 + len(arrays)),
        out_specs=(hbm,) * len(arrays),
        input_output_aliases={1 + i: i for i in range(len(arrays))},
        compiler_params=pltpu.CompilerParams(vmem_limit_bytes=2**20),
    )(step, *arrays)


def moved(x, dy, dx, dcore):
    pairs = []
    for y in range(4):
        for x_hi in range(2):
            for core in range(2):
                to = ((y + dy) % 4) * 4 + (x_hi ^ dx) * 2 + (core ^ dcore)
                pairs.append((y * 4 + x_hi * 2 + core, to))
    return lax.ppermute(x, "blk", pairs)


def per_device(query, keys, values, positions):
    n_blk, n_head = lax.axis_size("blk"), lax.axis_size("head")
    blk, head = lax.axis_index("blk"), lax.axis_index("head")
    rows = query.shape[0]
    quarters = SEGLEN // rows

    per = rows // n_blk

    def spread(x):
        return jnp.transpose(x.reshape(n_blk, per, n_head, -1), (0, 2, 1, 3))

    def longest(x):
        heads = x.shape[1] // HEAD_DIM
        same = np.arange(x.shape[1])[:, None] // HEAD_DIM == np.arange(heads)
        squares = jnp.dot(x * x, jnp.asarray(same, bf16), preferred_element_type=f32)
        return jnp.max(squares.reshape(rows, n_head, -1), axis=(0, 2)) * 1.02

    place = jnp.where(head < quarters, positions[0], positions[SEGLEN])
    place = lax.div(place, SEGLEN).astype(f32)
    lane = lax.broadcasted_iota(i32, (n_head, 128), 1)
    tag = jnp.where(lane == 0, place, jnp.where(lane == 1, longest(query)[:, None], longest(keys)[:, None]))
    tag = jnp.broadcast_to(tag.astype(bf16)[None, :, None, :], (n_blk, n_head, per, 128))
    sent = jnp.concatenate([spread(query), spread(keys), spread(values), tag], axis=3)
    width = GROUP * HEAD_DIM
    sent = sent.reshape(n_blk * n_head, per, width + WIDE + 128)
    got = lax.all_to_all(sent, ("blk", "head"), split_axis=0, concat_axis=0, tiled=True)
    tags = got[:, 0, width + WIDE :].astype(f32)
    order = tags[::quarters, 0].astype(i32)
    most = jnp.max(tags[:, 1]) * jnp.max(tags[:, 2]) * (SCALE * SCALE)
    shifted = jnp.where(most <= SAFE * SAFE, 0, 1)
    listed = jnp.asarray([q for q, _ in STEPS] + [k for _, k in STEPS], i32)
    offsets = [(0, 0, 0), (0, 0, 1), (0, 1, 0), (0, 1, 1), (-1, 0, 0), (1, 0, 0)]
    offsets += [(-1, 0, 1), (1, 0, 1), (-1, 1, 0), (1, 1, 0)]
    offsets += [(-1, 1, 1), (1, 1, 1), (2, 0, 0), (2, 1, 0), (2, 0, 1), (2, 1, 1)]
    first_row = 8 * jnp.stack([lax.rem(blk + 4 * dy + n_blk, n_blk) ^ (2 * dx + dcore) for dy, dx, dcore in offsets])
    common = jnp.stack([shifted, blk * 8] + [jnp.zeros_like(blk)] * 6)
    meta = jnp.concatenate([order, common, listed, first_row])
    got = got.reshape(n_blk * n_head * per, width + WIDE + 128)
    own = got[:, width : width + WIDE]

    x, own_core = moved(own, 0, 1, 0), moved(own, 0, 0, 1)
    own_up, own_down = moved(own, 1, 0, 0), moved(own, -1, 0, 0)
    call = attention_call(meta, 0, got, None, [own, own_core], False)
    stacked, state = call[0], call[1:]

    x, own_up, own_down = held(state[1], x, own_up, own_down)
    x_up, x_down, x_core = moved(x, 1, 0, 0), moved(x, -1, 0, 0), moved(x, 0, 0, 1)
    own_up_core, own_down_core = moved(own_up, 0, 0, 1), moved(own_down, 0, 0, 1)
    state = attention_call(meta, 2, stacked, state, [x, x_core, own_up, own_down], False)

    x_up, x_down, own_up = held(state[1], x_up, x_down, own_up)
    own_far, x_far = moved(own_up, 1, 0, 0), moved(x_down, -1, 0, 0)
    x_up_core, x_down_core = moved(x_up, 0, 0, 1), moved(x_down, 0, 0, 1)
    state = attention_call(meta, 6, stacked, state, [own_up_core, own_down_core, x_up, x_down], False)

    own_far, x_far = held(state[1], own_far, x_far)
    own_far_core, x_far_core = moved(own_far, 0, 0, 1), moved(x_far, 0, 0, 1)
    chunks = [x_up_core, x_down_core, own_far, x_far, own_far_core, x_far_core]
    out = attention_call(meta, 10, stacked, state, chunks, True)[-1]
    out = out.reshape(n_blk * n_head, per, GROUP * HEAD_DIM)
    back = lax.all_to_all(out, ("blk", "head"), split_axis=0, concat_axis=0, tiled=True)
    back = back.reshape(n_blk, n_head, per, GROUP * HEAD_DIM)
    return jnp.transpose(back, (0, 2, 1, 3)).reshape(rows, HEADS * HEAD_DIM)


def solution(mesh):
    placed = (
        P(("blk", "head"), None),
        P(("blk", "head"), None),
        P(("blk", "head"), None),
        P("blk"),
    )
    return jax.shard_map(
        per_device, mesh=mesh, in_specs=placed, out_specs=P(("blk", "head"), None), check_vma=False
    )
```

```python
import functools

import jax
import jax.numpy as jnp
import numpy as np
from jax import lax
from jax.experimental import pallas as pl
from jax.experimental.pallas import tpu as pltpu
from jax.sharding import PartitionSpec as P

HEADS = 32
KV_HEADS = 8
HEAD_DIM = 128
GROUP = HEADS // KV_HEADS
SEGLEN = 512
SEGS = 32
PART = SEGLEN // 16
TILE = GROUP * PART
ROWS = SEGS * TILE
QSEGS = 4
QB = QSEGS * TILE
BLOCKS = SEGS // QSEGS
UNROLL = 14
WIDE = 2 * HEAD_DIM
LOG2E = 1.4426950408889634
SCALE = HEAD_DIM**-0.5 * LOG2E
SAFE = 48.0
LOW = -1e30
NT = (((1,), (1,)), ((), ()))
bf16, f32, i32 = jnp.bfloat16, jnp.float32, jnp.int32

STEPS = [(b, b) for b in range(BLOCKS)] + [(q, k) for k in range(BLOCKS) for q in range(k + 1, BLOCKS)]


def attend(n, done, first, last, *refs):
    refs = list(refs)
    meta, q_ref = refs[:2]
    refs = refs[2:]
    if not first:
        acc_in, m_in = refs[:2]
        refs = refs[2:]
    chunks, refs = refs[:n], refs[n:]
    qs = refs.pop(0) if first else q_ref
    acc, m_out = refs[:2]
    refs = refs[2:]
    if last:
        out = refs.pop(0)
    kv, m_ref, s_scr, p_scr, q_pos, k_pos, m_sem = refs
    shifted = meta[SEGS]
    part = n * PART
    keys = QSEGS * part

    row = lax.broadcasted_iota(i32, (QB, 128), 0)
    place = lax.rem(row, PART)
    q_pos[...] = lax.div(row, TILE) * SEGLEN + lax.div(place, 8) * 128 + lax.rem(place, 8) + meta[SEGS + 1]
    column = lax.broadcasted_iota(i32, (8, keys), 1)
    within = sum(jnp.where(column >= i * part, 1, 0) for i in range(1, QSEGS))
    chunk = column - within * part
    offset = sum(jnp.where(lax.div(chunk, PART) == c, meta[SEGS + 8 + 2 * len(STEPS) + done + c], 0) for c in range(n))
    place = lax.rem(chunk, PART)
    k_pos[...] = within * SEGLEN + lax.div(place, 8) * 128 + lax.rem(place, 8) + offset
    kv[:, :, WIDE:] = jnp.ones((BLOCKS, keys, HEAD_DIM), bf16)

    def lay(s, _):
        p = meta[s]
        block, within = lax.div(p, QSEGS), lax.rem(p, QSEGS)
        rows = pl.ds(pl.multiple_of(s * PART, PART), PART)
        for c in range(n):
            to = pl.ds(pl.multiple_of(within * part + c * PART, PART), PART)
            kv[block, to, :WIDE] = chunks[c][rows, :]
        if first:
            for g in range(GROUP):
                to = pl.ds(pl.multiple_of(p * TILE + g * PART, PART), PART)
                qs[to, :] = q_ref[rows, g * HEAD_DIM : (g + 1) * HEAD_DIM]
        return 0

    lax.fori_loop(0, SEGS, lay, 0)

    def step_of(t):
        if isinstance(t, int):
            return STEPS[t]
        return meta[SEGS + 8 + t], meta[SEGS + 8 + len(STEPS) + t]

    def rows_of(block):
        return pl.ds(pl.multiple_of(block * QB, QB), QB)

    def scores(t):
        q_block, k_block = step_of(t)
        return lax.dot_general(
            qs[rows_of(q_block), :], kv[k_block, :, :HEAD_DIM], NT, preferred_element_type=f32
        )

    def seen(c):
        return k_pos[0:1, c : c + 128] <= q_pos[...]

    def weigh(t, slot):
        p_scr[slot] = jnp.exp2(scores(t) * SCALE).astype(bf16)

    def collect(t, slot):
        return jnp.dot(p_scr[slot], kv[step_of(t)[1], :, HEAD_DIM:], preferred_element_type=f32)

    halves = [(0, keys // 2), (QB // 2, keys)]

    def weigh_diagonal(t, slot):
        for start, width in halves:
            some = pl.ds(t * QB + start, QB // 2)
            found = lax.dot_general(qs[some, :], kv[t, :width, :HEAD_DIM], NT, preferred_element_type=f32)
            weights = jnp.exp2(found * SCALE)
            for c in range(0, width, 128):
                visible = k_pos[0:1, c : c + 128] <= q_pos[start : start + QB // 2, :]
                kept = jnp.where(visible, weights[:, c : c + 128], 0.0)
                p_scr[slot, start : start + QB // 2, c : c + 128] = kept.astype(bf16)

    def collect_diagonal(t, slot):
        for start, width in halves:
            some = pl.ds(t * QB + start, QB // 2)
            weights = p_scr[slot, start : start + QB // 2, :width]
            added = jnp.dot(weights, kv[t, :width, HEAD_DIM:], preferred_element_type=f32)
            acc[some, :] = added if first else acc_in[some, :] + added

    @pl.when(shifted == 0)
    def _():
        for t in range(BLOCKS):
            weigh_diagonal(t, t % 2)
            if t:
                collect_diagonal(t - 1, (t - 1) % 2)
        collect_diagonal(BLOCKS - 1, (BLOCKS - 1) % 2)
        weigh(BLOCKS, 0)

        def body(u, _):
            for r in range(UNROLL):
                t = BLOCKS + u * UNROLL + r
                weigh(jnp.minimum(t + 1, len(STEPS) - 1), (r + 1) % 2)
                acc[rows_of(step_of(t)[0]), :] += collect(t, r % 2)
            return 0

        assert (len(STEPS) - BLOCKS) % UNROLL == 0
        lax.fori_loop(0, (len(STEPS) - BLOCKS) // UNROLL, body, 0)

    @pl.when(shifted != 0)
    def _():
        if first:
            m_ref[...] = jnp.full_like(m_ref, LOW)
            acc[...] = jnp.zeros_like(acc)
        else:
            copy = pltpu.make_async_copy(m_in, m_ref, m_sem)
            copy.start()
            copy.wait()
            acc[...] = acc_in[...]

        def step(masked):
            def body(t, _):
                rows = rows_of(step_of(t)[0])
                s_scr[...] = scores(t) * SCALE
                if masked:
                    for c in range(0, keys, 128):
                        s_scr[:, c : c + 128] = jnp.where(seen(c), s_scr[:, c : c + 128], LOW)
                before = m_ref[rows, :]
                now = jnp.maximum(before, jnp.max(s_scr[...], axis=1, keepdims=True))
                factor = jnp.exp2(before - now)
                m_ref[rows, :] = now
                for c in range(0, keys, 128):
                    p_scr[0, :, c : c + 128] = jnp.exp2(s_scr[:, c : c + 128] - now).astype(bf16)
                added = collect(t, 0)
                for c in (0, HEAD_DIM):
                    to = slice(c, c + HEAD_DIM)
                    acc[rows, to] = acc[rows, to] * factor + added[:, to]
                return 0

            return body

        lax.fori_loop(0, BLOCKS, step(True), 0)
        lax.fori_loop(BLOCKS, len(STEPS), step(False), 0)
        copy = pltpu.make_async_copy(m_ref, m_out, m_sem)
        copy.start()
        copy.wait()

    if last:
        def finish(s, _):
            p = meta[s]
            for g in range(GROUP):
                rows = pl.ds(pl.multiple_of(p * TILE + g * PART, PART), PART)
                out[pl.ds(pl.multiple_of(s * PART, PART), PART), g * HEAD_DIM : (g + 1) * HEAD_DIM] = (
                    acc[rows, :HEAD_DIM] / acc[rows, HEAD_DIM:]
                ).astype(bf16)
            return 0

        lax.fori_loop(0, SEGS, finish, 0)


def attention_call(meta, done, q, state, chunks, last):
    first, n = state is None, len(chunks)
    keys = QSEGS * n * PART
    vmem, hbm = pl.BlockSpec(memory_space=pltpu.VMEM), pl.BlockSpec(memory_space=pl.ANY)
    smem = pl.BlockSpec(memory_space=pltpu.SMEM)
    operands = [meta, q] + ([] if first else list(state)) + chunks
    in_specs = [smem, vmem] + ([] if first else [vmem, hbm]) + [vmem] * n
    out_shape = [jax.ShapeDtypeStruct((ROWS, WIDE), f32), jax.ShapeDtypeStruct((ROWS, 128), f32)]
    out_specs = [vmem, hbm]
    if first:
        out_shape = [jax.ShapeDtypeStruct((ROWS, HEAD_DIM), bf16)] + out_shape
        out_specs = [vmem] + out_specs
    if last:
        out_shape = out_shape + [jax.ShapeDtypeStruct((SEGS * PART, GROUP * HEAD_DIM), bf16)]
        out_specs = out_specs + [vmem]
    return pl.pallas_call(
        functools.partial(attend, n, done, first, last),
        out_shape=tuple(out_shape),
        in_specs=in_specs,
        out_specs=tuple(out_specs),
        input_output_aliases={} if first else {2: 0},
        scratch_shapes=[
            pltpu.VMEM((BLOCKS, keys, WIDE + HEAD_DIM), bf16),
            pltpu.VMEM((ROWS, 128), f32),
            pltpu.VMEM((QB, keys), f32),
            pltpu.VMEM((2, QB, keys), bf16),
            pltpu.VMEM((QB, 128), i32),
            pltpu.VMEM((8, keys), i32),
            pltpu.SemaphoreType.DMA,
        ],
        compiler_params=pltpu.CompilerParams(vmem_limit_bytes=36 * 2**20),
        cost_estimate=pl.CostEstimate(
            flops=len(STEPS) * QB * keys * 4 * WIDE,
            bytes_accessed=n * SEGS * PART * 512 + ROWS * WIDE * 4,
            transcendentals=len(STEPS) * QB * keys,
        ),
    )(*operands)


def tags_of(query, keys, positions, tag):
    lane = lax.broadcasted_iota(i32, (1, 128), 1)
    second = SEGLEN // 128
    places = [lax.shift_right_logical(positions[i : i + 1, 0:1], SEGLEN.bit_length() - 1) for i in (0, second)]

    def longest(ref, start, n):
        most = None
        for i in range(start, start + n):
            x = ref[:, i * HEAD_DIM : (i + 1) * HEAD_DIM].astype(f32)
            length = jnp.sum(x * x, axis=1, keepdims=True)
            most = length if most is None else jnp.maximum(most, length)
        return jnp.max(most, axis=0, keepdims=True) * 1.02

    for head in range(KV_HEADS):
        row = jnp.where(lane == 0, longest(query, head * GROUP, GROUP), longest(keys, head, 1))
        for i, place in enumerate(places):
            row = jnp.where(lane == 2 + i, place.astype(f32), row)
        tag[head : head + 1, :] = row


def held(step, *arrays):
    hbm = pl.BlockSpec(memory_space=pl.ANY)

    def nothing(*refs):
        del refs

    return pl.pallas_call(
        nothing,
        out_shape=tuple(jax.ShapeDtypeStruct(a.shape, a.dtype) for a in arrays),
        in_specs=[hbm] * (1 + len(arrays)),
        out_specs=(hbm,) * len(arrays),
        input_output_aliases={1 + i: i for i in range(len(arrays))},
        compiler_params=pltpu.CompilerParams(vmem_limit_bytes=2**20),
    )(step, *arrays)


def moved(x, dy, dx, dcore):
    pairs = []
    for y in range(4):
        for x_hi in range(2):
            for core in range(2):
                to = ((y + dy) % 4) * 4 + (x_hi ^ dx) * 2 + (core ^ dcore)
                pairs.append((y * 4 + x_hi * 2 + core, to))
    return lax.ppermute(x, "blk", pairs)


def per_device(query, keys, values, positions):
    n_blk, n_head = lax.axis_size("blk"), lax.axis_size("head")
    blk = lax.axis_index("blk")
    rows = query.shape[0]

    per = rows // n_blk

    def spread(x):
        return jnp.transpose(x.reshape(n_blk, per, n_head, -1), (0, 2, 1, 3))

    tag = pl.pallas_call(
        tags_of,
        out_shape=jax.ShapeDtypeStruct((n_head, 128), f32),
        in_specs=[pl.BlockSpec(memory_space=pltpu.VMEM)] * 3,
        out_specs=pl.BlockSpec(memory_space=pltpu.VMEM),
        compiler_params=pltpu.CompilerParams(vmem_limit_bytes=8 * 2**20),
    )(query, keys, positions.reshape(-1, 128))
    tag = jnp.broadcast_to(tag.astype(bf16)[None, :, None, :], (n_blk, n_head, per, 128))
    sent = jnp.concatenate([spread(query), spread(keys), spread(values), tag], axis=3)
    width = GROUP * HEAD_DIM
    sent = sent.reshape(n_blk * n_head, per, width + WIDE + 128)
    got = lax.all_to_all(sent, ("blk", "head"), split_axis=0, concat_axis=0, tiled=True)
    tags = got[:, 0, width + WIDE :].astype(f32)
    order = tags[::n_head, 2:4].reshape(-1).astype(i32)
    most = jnp.max(tags[:, 0]) * jnp.max(tags[:, 1]) * (SCALE * SCALE)
    shifted = jnp.where(most <= SAFE * SAFE, 0, 1)
    listed = jnp.asarray([q for q, _ in STEPS] + [k for _, k in STEPS], i32)
    offsets = [(0, 0, 0), (0, 0, 1), (0, 1, 0), (0, 1, 1), (-1, 0, 0), (1, 0, 0)]
    offsets += [(-1, 0, 1), (1, 0, 1), (-1, 1, 0), (1, 1, 0), (2, 0, 0), (-1, 1, 1)]
    offsets += [(1, 1, 1), (2, 0, 1), (2, 1, 0), (2, 1, 1)]
    first_row = 8 * jnp.stack([lax.rem(blk + 4 * dy + n_blk, n_blk) ^ (2 * dx + dcore) for dy, dx, dcore in offsets])
    common = jnp.stack([shifted, blk * 8] + [jnp.zeros_like(blk)] * 6)
    meta = jnp.concatenate([order, common, listed, first_row])
    got = got.reshape(n_blk * n_head * per, width + WIDE + 128)
    own = got[:, width : width + WIDE]

    x, own_core = moved(own, 0, 1, 0), moved(own, 0, 0, 1)
    own_up, own_down = moved(own, 1, 0, 0), moved(own, -1, 0, 0)
    call = attention_call(meta, 0, got, None, [own, own_core], False)
    stacked, state = call[0], call[1:]

    x, own_up, own_down = held(state[1], x, own_up, own_down)
    x_core, own_up_core, own_down_core = moved(x, 0, 0, 1), moved(own_up, 0, 0, 1), moved(own_down, 0, 0, 1)
    x_up, x_down, own_far = moved(own_up, 0, 1, 0), moved(x, -1, 0, 0), moved(own_up, 1, 0, 0)
    state = attention_call(meta, 2, stacked, state, [x, x_core, own_up, own_down], False)

    x_up, x_down, own_far = held(state[1], x_up, x_down, own_far)
    x_up_core, x_down_core, own_far_core = moved(x_up, 0, 0, 1), moved(x_down, 0, 0, 1), moved(own_far, 0, 0, 1)
    x_far = moved(own_far, 0, 1, 0)
    chunks = [own_up_core, own_down_core, x_up, x_down, own_far, x_up_core]
    state = attention_call(meta, 6, stacked, state, chunks, False)

    x_far = held(state[1], x_far)[0]
    x_far_core = moved(x_far, 0, 0, 1)
    chunks = [x_down_core, own_far_core, x_far, x_far_core]
    out = attention_call(meta, 12, stacked, state, chunks, True)[-1]
    out = out.reshape(n_blk * n_head, per, GROUP * HEAD_DIM)
    back = lax.all_to_all(out, ("blk", "head"), split_axis=0, concat_axis=0, tiled=True)
    back = back.reshape(n_blk, n_head, per, GROUP * HEAD_DIM)
    return jnp.transpose(back, (0, 2, 1, 3)).reshape(rows, HEADS * HEAD_DIM)


def solution(mesh):
    placed = (
        P(("blk", "head"), None),
        P(("blk", "head"), None),
        P(("blk", "head"), None),
        P("blk"),
    )
    return jax.shard_map(
        per_device, mesh=mesh, in_specs=placed, out_specs=P(("blk", "head"), None), check_vma=False
    )
```

```python
import functools

import jax
import jax.numpy as jnp
import numpy as np
from jax import lax
from jax.experimental import pallas as pl
from jax.experimental.pallas import tpu as pltpu
from jax.sharding import PartitionSpec as P

HEADS = 32
KV_HEADS = 8
HEAD_DIM = 128
GROUP = HEADS // KV_HEADS
SEGLEN = 512
SEGS = 32
PART = SEGLEN // 16
TILE = GROUP * PART
ROWS = SEGS * TILE
QSEGS = 4
QB = QSEGS * TILE
BLOCKS = SEGS // QSEGS
UNROLL = 14
WIDE = 2 * HEAD_DIM
LOG2E = 1.4426950408889634
SCALE = HEAD_DIM**-0.5 * LOG2E
SAFE = 48.0
LOW = -1e30
NT = (((1,), (1,)), ((), ()))
bf16, f32, i32 = jnp.bfloat16, jnp.float32, jnp.int32

STEPS = [(b, b) for b in range(BLOCKS)] + [(q, k) for k in range(BLOCKS) for q in range(k + 1, BLOCKS)]


def attend(n, done, first, last, *refs):
    refs = list(refs)
    meta, q_ref = refs[:2]
    refs = refs[2:]
    if not first:
        acc_in, m_in = refs[:2]
        refs = refs[2:]
    chunks, refs = refs[:n], refs[n:]
    qs = refs.pop(0) if first else q_ref
    acc, m_out = refs[:2]
    refs = refs[2:]
    if last:
        out = refs.pop(0)
    kv, m_ref, s_scr, p_scr, q_pos, k_pos, m_sem = refs
    shifted = meta[SEGS]
    part = n * PART
    keys = QSEGS * part

    row = lax.broadcasted_iota(i32, (QB, 128), 0)
    place = lax.rem(row, PART)
    q_pos[...] = lax.div(row, TILE) * SEGLEN + lax.div(place, 8) * 128 + lax.rem(place, 8) + meta[SEGS + 1]
    column = lax.broadcasted_iota(i32, (8, keys), 1)
    within = sum(jnp.where(column >= i * part, 1, 0) for i in range(1, QSEGS))
    chunk = column - within * part
    offset = sum(jnp.where(lax.div(chunk, PART) == c, meta[SEGS + 8 + 2 * len(STEPS) + done + c], 0) for c in range(n))
    place = lax.rem(chunk, PART)
    k_pos[...] = within * SEGLEN + lax.div(place, 8) * 128 + lax.rem(place, 8) + offset
    kv[:, :, WIDE:] = jnp.ones((BLOCKS, keys, HEAD_DIM), bf16)

    def lay(s, _):
        p = meta[s]
        block, within = lax.div(p, QSEGS), lax.rem(p, QSEGS)
        rows = pl.ds(pl.multiple_of(s * PART, PART), PART)
        for c in range(n):
            to = pl.ds(pl.multiple_of(within * part + c * PART, PART), PART)
            kv[block, to, :WIDE] = chunks[c][rows, :]
        if first:
            for g in range(GROUP):
                to = pl.ds(pl.multiple_of(p * TILE + g * PART, PART), PART)
                qs[to, :] = q_ref[rows, g * HEAD_DIM : (g + 1) * HEAD_DIM]
        return 0

    lax.fori_loop(0, SEGS, lay, 0)

    def step_of(t):
        if isinstance(t, int):
            return STEPS[t]
        return meta[SEGS + 8 + t], meta[SEGS + 8 + len(STEPS) + t]

    def rows_of(block):
        return pl.ds(pl.multiple_of(block * QB, QB), QB)

    def scores(t):
        q_block, k_block = step_of(t)
        return lax.dot_general(
            qs[rows_of(q_block), :], kv[k_block, :, :HEAD_DIM], NT, preferred_element_type=f32
        )

    def seen(c):
        return k_pos[0:1, c : c + 128] <= q_pos[...]

    def weigh(t, slot):
        p_scr[slot] = jnp.exp2(scores(t) * SCALE).astype(bf16)

    def collect(t, slot):
        return jnp.dot(p_scr[slot], kv[step_of(t)[1], :, HEAD_DIM:], preferred_element_type=f32)

    halves = [(0, keys // 2), (QB // 2, keys)]

    def weigh_diagonal(t, slot):
        for start, width in halves:
            some = pl.ds(t * QB + start, QB // 2)
            found = lax.dot_general(qs[some, :], kv[t, :width, :HEAD_DIM], NT, preferred_element_type=f32)
            weights = jnp.exp2(found * SCALE)
            for c in range(0, width, 128):
                visible = k_pos[0:1, c : c + 128] <= q_pos[start : start + QB // 2, :]
                kept = jnp.where(visible, weights[:, c : c + 128], 0.0)
                p_scr[slot, start : start + QB // 2, c : c + 128] = kept.astype(bf16)

    def collect_diagonal(t, slot):
        for start, width in halves:
            some = pl.ds(t * QB + start, QB // 2)
            weights = p_scr[slot, start : start + QB // 2, :width]
            added = jnp.dot(weights, kv[t, :width, HEAD_DIM:], preferred_element_type=f32)
            acc[some, :] = added if first else acc_in[some, :] + added

    @pl.when(shifted == 0)
    def _():
        for t in range(BLOCKS):
            weigh_diagonal(t, t % 2)
            if t:
                collect_diagonal(t - 1, (t - 1) % 2)
        collect_diagonal(BLOCKS - 1, (BLOCKS - 1) % 2)
        weigh(BLOCKS, 0)

        def body(u, _):
            for r in range(UNROLL):
                t = BLOCKS + u * UNROLL + r
                weigh(jnp.minimum(t + 1, len(STEPS) - 1), (r + 1) % 2)
                acc[rows_of(step_of(t)[0]), :] += collect(t, r % 2)
            return 0

        assert (len(STEPS) - BLOCKS) % UNROLL == 0
        lax.fori_loop(0, (len(STEPS) - BLOCKS) // UNROLL, body, 0)

    @pl.when(shifted != 0)
    def _():
        if first:
            m_ref[...] = jnp.full_like(m_ref, LOW)
            acc[...] = jnp.zeros_like(acc)
        else:
            copy = pltpu.make_async_copy(m_in, m_ref, m_sem)
            copy.start()
            copy.wait()
            acc[...] = acc_in[...]

        def step(masked):
            def body(t, _):
                rows = rows_of(step_of(t)[0])
                s_scr[...] = scores(t) * SCALE
                if masked:
                    for c in range(0, keys, 128):
                        s_scr[:, c : c + 128] = jnp.where(seen(c), s_scr[:, c : c + 128], LOW)
                before = m_ref[rows, :]
                now = jnp.maximum(before, jnp.max(s_scr[...], axis=1, keepdims=True))
                factor = jnp.exp2(before - now)
                m_ref[rows, :] = now
                for c in range(0, keys, 128):
                    p_scr[0, :, c : c + 128] = jnp.exp2(s_scr[:, c : c + 128] - now).astype(bf16)
                added = collect(t, 0)
                for c in (0, HEAD_DIM):
                    to = slice(c, c + HEAD_DIM)
                    acc[rows, to] = acc[rows, to] * factor + added[:, to]
                return 0

            return body

        lax.fori_loop(0, BLOCKS, step(True), 0)
        lax.fori_loop(BLOCKS, len(STEPS), step(False), 0)
        copy = pltpu.make_async_copy(m_ref, m_out, m_sem)
        copy.start()
        copy.wait()

    if last:
        def finish(s, _):
            p = meta[s]
            for g in range(GROUP):
                rows = pl.ds(pl.multiple_of(p * TILE + g * PART, PART), PART)
                out[pl.ds(pl.multiple_of(s * PART, PART), PART), g * HEAD_DIM : (g + 1) * HEAD_DIM] = (
                    acc[rows, :HEAD_DIM] / acc[rows, HEAD_DIM:]
                ).astype(bf16)
            return 0

        lax.fori_loop(0, SEGS, finish, 0)


def attention_call(meta, done, q, state, chunks, last):
    first, n = state is None, len(chunks)
    keys = QSEGS * n * PART
    vmem, hbm = pl.BlockSpec(memory_space=pltpu.VMEM), pl.BlockSpec(memory_space=pl.ANY)
    smem = pl.BlockSpec(memory_space=pltpu.SMEM)
    operands = [meta, q] + ([] if first else list(state)) + chunks
    in_specs = [smem, vmem] + ([] if first else [vmem, hbm]) + [vmem] * n
    out_shape = [jax.ShapeDtypeStruct((ROWS, WIDE), f32), jax.ShapeDtypeStruct((ROWS, 128), f32)]
    out_specs = [vmem, hbm]
    if first:
        out_shape = [jax.ShapeDtypeStruct((ROWS, HEAD_DIM), bf16)] + out_shape
        out_specs = [vmem] + out_specs
    if last:
        out_shape = out_shape + [jax.ShapeDtypeStruct((SEGS * PART, GROUP * HEAD_DIM), bf16)]
        out_specs = out_specs + [vmem]
    return pl.pallas_call(
        functools.partial(attend, n, done, first, last),
        out_shape=tuple(out_shape),
        in_specs=in_specs,
        out_specs=tuple(out_specs),
        input_output_aliases={} if first else {2: 0},
        scratch_shapes=[
            pltpu.VMEM((BLOCKS, keys, WIDE + HEAD_DIM), bf16),
            pltpu.VMEM((ROWS, 128), f32),
            pltpu.VMEM((QB, keys), f32),
            pltpu.VMEM((2, QB, keys), bf16),
            pltpu.VMEM((QB, 128), i32),
            pltpu.VMEM((8, keys), i32),
            pltpu.SemaphoreType.DMA,
        ],
        compiler_params=pltpu.CompilerParams(vmem_limit_bytes=36 * 2**20),
        cost_estimate=pl.CostEstimate(
            flops=len(STEPS) * QB * keys * 4 * WIDE,
            bytes_accessed=n * SEGS * PART * 512 + ROWS * WIDE * 4,
            transcendentals=len(STEPS) * QB * keys,
        ),
    )(*operands)


def held(step, *arrays):
    hbm = pl.BlockSpec(memory_space=pl.ANY)

    def nothing(*refs):
        del refs

    return pl.pallas_call(
        nothing,
        out_shape=tuple(jax.ShapeDtypeStruct(a.shape, a.dtype) for a in arrays),
        in_specs=[hbm] * (1 + len(arrays)),
        out_specs=(hbm,) * len(arrays),
        input_output_aliases={1 + i: i for i in range(len(arrays))},
        compiler_params=pltpu.CompilerParams(vmem_limit_bytes=2**20),
    )(step, *arrays)


def moved(x, dy, dx, dcore):
    pairs = []
    for y in range(4):
        for x_hi in range(2):
            for core in range(2):
                to = ((y + dy) % 4) * 4 + (x_hi ^ dx) * 2 + (core ^ dcore)
                pairs.append((y * 4 + x_hi * 2 + core, to))
    return lax.ppermute(x, "blk", pairs)


def per_device(query, keys, values, positions):
    n_blk, n_head = lax.axis_size("blk"), lax.axis_size("head")
    blk, head = lax.axis_index("blk"), lax.axis_index("head")
    rows = query.shape[0]
    quarters = SEGLEN // rows

    per = rows // n_blk

    def spread(x):
        return jnp.transpose(x.reshape(n_blk, per, n_head, -1), (0, 2, 1, 3))

    def longest(x):
        heads = x.shape[1] // HEAD_DIM
        same = np.arange(x.shape[1])[:, None] // HEAD_DIM == np.arange(heads)
        squares = jnp.dot(x * x, jnp.asarray(same, bf16), preferred_element_type=f32)
        return jnp.max(squares.reshape(rows, n_head, -1), axis=(0, 2)) * 1.02

    place = jnp.where(head < quarters, positions[0], positions[SEGLEN])
    place = lax.div(place, SEGLEN).astype(f32)
    lane = lax.broadcasted_iota(i32, (n_head, 128), 1)
    tag = jnp.where(lane == 0, place, jnp.where(lane == 1, longest(query)[:, None], longest(keys)[:, None]))
    tag = jnp.broadcast_to(tag.astype(bf16)[None, :, None, :], (n_blk, n_head, per, 128))
    sent = jnp.concatenate([spread(query), spread(keys), spread(values), tag], axis=3)
    width = GROUP * HEAD_DIM
    sent = sent.reshape(n_blk * n_head, per, width + WIDE + 128)
    got = lax.all_to_all(sent, ("blk", "head"), split_axis=0, concat_axis=0, tiled=True)
    tags = got[:, 0, width + WIDE :].astype(f32)
    order = tags[::quarters, 0].astype(i32)
    most = jnp.max(tags[:, 1]) * jnp.max(tags[:, 2]) * (SCALE * SCALE)
    shifted = jnp.where(most <= SAFE * SAFE, 0, 1)
    listed = jnp.asarray([q for q, _ in STEPS] + [k for _, k in STEPS], i32)
    offsets = [(0, 0, 0), (0, 0, 1), (0, 1, 0), (0, 1, 1), (-1, 0, 0), (1, 0, 0)]
    offsets += [(-1, 0, 1), (1, 0, 1), (-1, 1, 0), (1, 1, 0), (2, 0, 0), (-1, 1, 1)]
    offsets += [(1, 1, 1), (2, 0, 1), (2, 1, 0), (2, 1, 1)]
    first_row = 8 * jnp.stack([lax.rem(blk + 4 * dy + n_blk, n_blk) ^ (2 * dx + dcore) for dy, dx, dcore in offsets])
    common = jnp.stack([shifted, blk * 8] + [jnp.zeros_like(blk)] * 6)
    meta = jnp.concatenate([order, common, listed, first_row])
    got = got.reshape(n_blk * n_head * per, width + WIDE + 128)
    own = got[:, width : width + WIDE]

    x, own_core = moved(own, 0, 1, 0), moved(own, 0, 0, 1)
    own_up, own_down = moved(own, 1, 0, 0), moved(own, -1, 0, 0)
    call = attention_call(meta, 0, got, None, [own, own_core], False)
    stacked, state = call[0], call[1:]

    x, own_up, own_down = held(state[1], x, own_up, own_down)
    x_core, own_up_core, own_down_core = moved(x, 0, 0, 1), moved(own_up, 0, 0, 1), moved(own_down, 0, 0, 1)
    x_up, x_down, own_far = moved(own_up, 0, 1, 0), moved(x, -1, 0, 0), moved(own_up, 1, 0, 0)
    state = attention_call(meta, 2, stacked, state, [x, x_core, own_up, own_down], False)

    x_up, x_down, own_far = held(state[1], x_up, x_down, own_far)
    x_up_core, x_down_core, own_far_core = moved(x_up, 0, 0, 1), moved(x_down, 0, 0, 1), moved(own_far, 0, 0, 1)
    x_far = moved(own_far, 0, 1, 0)
    chunks = [own_up_core, own_down_core, x_up, x_down, own_far, x_up_core]
    state = attention_call(meta, 6, stacked, state, chunks, False)

    x_far = held(state[1], x_far)[0]
    x_far_core = moved(x_far, 0, 0, 1)
    chunks = [x_down_core, own_far_core, x_far, x_far_core]
    out = attention_call(meta, 12, stacked, state, chunks, True)[-1]
    out = out.reshape(n_blk * n_head, per, GROUP * HEAD_DIM)
    back = lax.all_to_all(out, ("blk", "head"), split_axis=0, concat_axis=0, tiled=True)
    back = back.reshape(n_blk, n_head, per, GROUP * HEAD_DIM)
    return jnp.transpose(back, (0, 2, 1, 3)).reshape(rows, HEADS * HEAD_DIM)


def solution(mesh):
    placed = (
        P(("blk", "head"), None),
        P(("blk", "head"), None),
        P(("blk", "head"), None),
        P("blk"),
    )
    return jax.shard_map(
        per_device, mesh=mesh, in_specs=placed, out_specs=P(("blk", "head"), None), check_vma=False
    )
```
